32 devices in a mesh: blk: 16 (over z, y, core), grp: 2 (over x).
Axes of the slice: x: 2, y: 2, z: 4, core: 2. Of those that a mesh axis runs over, the one named last changes fastest.
Arguments:
- occupied: bfloat16 [2048, 1024], P('blk'), may hold values from -6 to 6
- integrals: bfloat16 [16, 2, 3, 64, 4096], P('blk', 'grp'), may hold values from -0.75 to 0.75
- metric_inv: bfloat16 [16384, 1024], P('blk')
- pattern: int32 [16, 2, 3, 4], P('blk', 'grp'), may hold values from 0 to 15, as said below
- support: int32 [16, 8], P('blk'), may hold values from 0 to 1023, as said below
Outputs:
- exchange: float32 [2048, 128], P(('blk', 'grp'))
The draws below stay inside these ranges and needn't reach their ends.
Inputs may be any that keep to these rules, and one draw needn't show every extreme that they name: Field 0 of every slot of pattern[r, g] is a region within distance 3 of r along the closed chain of 16 regions; field 1 is below 2; field 2 is below 16; field 3 is 1 on a leading run of slots and 0 after it, and in every draw some basis block has all 3 slots live. `support`: the 8 orbitals of one region are distinct.
All inputs are finite; a program needn't handle non-finite values.
Results may differ from the reference program's by a relative error of at most 0.0045.
Values may be sent and summed in bfloat16 or wider, within the bound.
A program may use at most 64 MiB of HBM per device.

```python
import math
import jax
import jax.numpy as jnp
from jax import lax

NOCC = 1024
BF = 64
AB = 64
AUXR = 1024
OSUP = 8
NT = 3
REACH = 3
REGIONS = 16
RB = 128
BASIS = 2048


def draw_metric_inv(key, part):
    key_diag, key_noise = jax.random.split(key)
    scale = 1.0 / math.sqrt(OSUP * AUXR)
    diagonal = jnp.exp(jax.random.uniform(key_diag, (REGIONS, AUXR), jnp.float32, 0.0, math.log(2.0)))
    noise_part = jax.random.normal(key_noise, (REGIONS, AUXR, AUXR), jnp.float32)
    mirrored = (noise_part + jnp.swapaxes(noise_part, 1, 2)) * (0.4 / math.sqrt(2.0 * AUXR))
    identity = (jnp.arange(AUXR)[:, None] == jnp.arange(AUXR)[None, :]).astype(jnp.float32)
    matrix = (diagonal[:, :, None] * identity[None] + mirrored) * scale
    return matrix.reshape(REGIONS * AUXR, AUXR).astype(jnp.bfloat16)


def draw_pattern(key, part):
    key_off, key_block, key_aux, key_live, key_full = jax.random.split(key, 5)
    groups = RB // BF
    shape = (REGIONS, groups, NT)
    region_ids = jnp.arange(REGIONS, dtype=jnp.int32)[:, None, None]
    offsets = jax.random.randint(key_off, shape, -REACH, REACH + 1, dtype=jnp.int32)
    source = (region_ids + offsets + REGIONS) % REGIONS
    basis_block = jax.random.randint(key_block, shape, 0, groups, dtype=jnp.int32)
    aux_block = jax.random.randint(key_aux, shape, 0, AUXR // AB, dtype=jnp.int32)
    live_count = jax.random.randint(key_live, (REGIONS, groups, 1), 1, NT + 1, dtype=jnp.int32)
    full_slot = jax.random.randint(key_full, (), 0, REGIONS * groups, dtype=jnp.int32)
    device_ids = jnp.arange(REGIONS * groups, dtype=jnp.int32).reshape(REGIONS, groups, 1)
    live_count = jnp.where(device_ids == full_slot, NT, live_count)
    live_flag = (jnp.arange(NT, dtype=jnp.int32)[None, None, :] < live_count).astype(jnp.int32)
    return jnp.stack([source, basis_block, aux_block, live_flag], axis=-1)


def draw_support(key, part):
    region_keys = jax.random.split(key, REGIONS)
    chosen = jax.vmap(lambda region_key: jax.random.permutation(region_key, NOCC)[:OSUP])(region_keys)
    chosen = chosen.astype(jnp.int32)
    picked_region = jax.random.randint(jax.random.fold_in(key, 7), (), 0, REGIONS, dtype=jnp.int32)
    region_ids = jnp.arange(REGIONS, dtype=jnp.int32)[:, None]
    highest = (chosen - chosen[:, :1] + NOCC - 1) % NOCC
    lowest = (chosen - chosen[:, :1] + NOCC) % NOCC
    result = jnp.where(region_ids == picked_region, highest, chosen)
    result = jnp.where(region_ids == (picked_region + 1) % REGIONS, lowest, result)
    return result


def levels(stream_key, dims, pieces, low, largest):
    level = 1.0
    for axis_at, parts in pieces:
        heights = jax.random.uniform(jax.random.fold_in(jax.random.fold_in(stream_key, 6), axis_at), (parts,), jnp.float32, low / len(pieces), largest / len(pieces))
        level = level * jnp.repeat(jnp.exp(heights), dims[axis_at] // parts).reshape((-1,) + (1,) * (len(dims) - 1 - axis_at))
    return level


def scatter_about(own_key, dims, scale, limit, cuts=(), kind=jnp.bfloat16):
    values = jax.random.normal(own_key, dims, jnp.float32) * scale
    if len(cuts) > 0:
        values = levels(own_key, dims, cuts, -0.22, 0.18) * values
    return jnp.clip(values, min=-limit, max=limit).astype(kind)


def setup_inputs(seed: int = 0) -> dict:
    key_list = jax.random.split(jax.random.key(seed), 6)
    occupied = scatter_about(key_list[0], (BASIS, NOCC), 1.0, 6.0, ((0, 16),))
    integrals = scatter_about(key_list[1], (REGIONS, RB // BF, NT, BF, BF * AB), 0.125, 0.75, ((0, 16), (1, 2)))
    metric_inv = draw_metric_inv(jax.random.fold_in(key_list[5], 71), 0)
    pattern = draw_pattern(jax.random.fold_in(key_list[5], 71), 0)
    support = draw_support(jax.random.fold_in(key_list[5], 71), 0)
    return {"occupied": occupied, "integrals": integrals, "metric_inv": metric_inv, "pattern": pattern, "support": support}


def reference(occupied, integrals, metric_inv, pattern, support):
    groups = RB // BF
    aux_blocks = AUXR // AB

    def region_rows(region):
        orbitals = support[region]
        tile_stack = integrals[region]
        slot_table = pattern[region]

        def tile_product(slot_fields, tile_data):
            first_row = (slot_fields[0] * RB + slot_fields[1] * BF).astype(jnp.int32)
            basis_rows = lax.dynamic_slice_in_dim(occupied, first_row, BF, 0)
            picked = jnp.take(basis_rows, orbitals, axis=1).astype(jnp.float32)
            return jnp.einsum("mi,mx->ix", picked, tile_data.astype(jnp.float32))

        def slot_weight(slot_fields):
            weight = (jnp.arange(aux_blocks, dtype=jnp.int32) == slot_fields[2]).astype(jnp.float32)
            return weight * slot_fields[3].astype(jnp.float32)

        products = jax.vmap(jax.vmap(tile_product))(slot_table, tile_stack)
        weights = jax.vmap(jax.vmap(slot_weight))(slot_table)
        summed = jnp.einsum("gta,gtix->gaix", weights, products)
        half_coef = summed.reshape(groups, aux_blocks, OSUP, BF, AB).transpose(0, 2, 3, 1, 4)
        half_coef = half_coef.reshape(groups, OSUP, BF, AUXR).astype(jnp.bfloat16)
        inverse = lax.dynamic_slice_in_dim(metric_inv, (region * AUXR).astype(jnp.int32), AUXR, 0)
        fitted = jnp.einsum("ginp,pq->ginq", half_coef.astype(jnp.float32), inverse.astype(jnp.float32))
        fitted = fitted.astype(jnp.bfloat16)
        exchange_block = jnp.einsum("ginq,himq->gnhm", half_coef.astype(jnp.float32), fitted.astype(jnp.float32))
        return exchange_block.reshape(RB, RB)

    blocks = lax.map(region_rows, jnp.arange(REGIONS, dtype=jnp.int32))
    return blocks.reshape(REGIONS * RB, RB)
```

```python
import functools

import jax
import jax.numpy as jnp
from jax import lax
from jax.experimental import pallas as pl
from jax.experimental.pallas import tpu as pltpu
from jax.sharding import PartitionSpec as P

BF = 64
AB = 64
AUXR = 1024
OSUP = 8
REACH = 3
LANES = 128
PAIR = LANES // BF
HALF = OSUP // PAIR
NEAR = tuple(d for d in range(-REACH, REACH + 1) if d != 0)
MESH = pl.DeviceIdType.MESH
NT_DIMS = (((1,), (1,)), ((), ()))


def iota(shape, dim):
    return lax.broadcasted_iota(jnp.int32, shape, dim)


def splat_rows(values):
    rows = iota((8, LANES), 0)
    tile = jnp.zeros((8, LANES), jnp.int32)
    for at, value in enumerate(values):
        tile = jnp.where(rows == at, value, tile)
    return tile


def kernel(
    regions, groups, occ_hbm, int_hbm, met_hbm, pat, sup, out_ref,
    occ, ints, met, mcol, m2, kbuf, my_sup, my_pat, sups, pats, picked, sel,
    comp, mixed, half, blocks,
    load_sem, sup_send, sup_recv, pat_send, pat_recv, sel_send, sel_recv, half_send, half_recv,
):
    slots = int_hbm.shape[2]
    rows = occ.shape[0]
    me = lax.axis_index("blk")
    mine = lax.axis_index("grp")
    near = [lax.rem(me + (d + regions), regions) for d in NEAR]
    peers = [lax.rem(mine + j, groups) for j in range(1, groups)]
    count = len(NEAR)

    loads = [
        pltpu.make_async_copy(occ_hbm, occ, load_sem.at[0]),
        pltpu.make_async_copy(met_hbm, met, load_sem.at[1]),
    ]
    for t in range(slots):
        loads.append(
            pltpu.make_async_copy(int_hbm.at[0, 0, t], ints.at[pl.ds(t * BF, BF)], load_sem.at[2 + t])
        )

    barrier = pltpu.get_barrier_semaphore()
    for region in near:
        pl.semaphore_signal(barrier, inc=1, device_id={"blk": region}, device_id_type=MESH)
    for peer in peers:
        pl.semaphore_signal(barrier, inc=1, device_id={"grp": peer}, device_id_type=MESH)
    for load in loads:
        load.start()

    aux = [pat[t, 0, 2] for t in range(slots)]
    my_sup[...] = splat_rows([sup[0, i] for i in range(OSUP)])
    my_pat[...] = splat_rows(aux)
    pats[0] = my_pat[...]
    pl.semaphore_wait(barrier, count + groups - 1)

    sup_out, pat_out = [], []
    for k, region in enumerate(near):
        copy = pltpu.make_async_remote_copy(
            src_ref=my_sup, dst_ref=sups.at[count - 1 - k], send_sem=sup_send.at[k],
            recv_sem=sup_recv.at[count - 1 - k], device_id={"blk": region}, device_id_type=MESH,
        )
        copy.start()
        sup_out.append(copy)
    for j, peer in enumerate(peers):
        copy = pltpu.make_async_remote_copy(
            src_ref=my_pat, dst_ref=pats.at[groups - 1 - j], send_sem=pat_send.at[j],
            recv_sem=pat_recv.at[groups - 2 - j], device_id={"grp": peer}, device_id_type=MESH,
        )
        copy.start()
        pat_out.append(copy)

    loads[1].wait()
    tall = iota((AUXR, LANES), 0)
    wide = iota((1, LANES), 1) % AB
    pick = jnp.concatenate(
        [(tall == aux[t] * AB + wide).astype(jnp.float32) for t in range(slots)], axis=1
    ).astype(jnp.bfloat16)
    mcol[...] = jnp.dot(met[...], pick, preferred_element_type=jnp.float32).astype(jnp.bfloat16)

    def one_hot(tile):
        lane = iota((8, LANES), 1)
        parts = [(lane + c * LANES == tile).astype(jnp.float32) for c in range(occ.shape[1] // LANES)]
        return jnp.concatenate(parts, axis=1)

    loads[0].wait()
    for k in range(count):
        sup_out[k].wait_recv()
    hot = jnp.concatenate([one_hot(sups[k]) for k in range(count)] + [one_hot(my_sup[...])], axis=0)
    chosen = lax.dot_general(
        hot.astype(jnp.bfloat16), occ[...], NT_DIMS, preferred_element_type=jnp.float32
    )
    for k in range(count):
        picked[k] = chosen[k * OSUP:(k + 1) * OSUP]
    sel[REACH] = chosen[count * OSUP:(count + 1) * OSUP]
    sel_out = []
    for k, region in enumerate(near):
        at = REACH - NEAR[k]
        copy = pltpu.make_async_remote_copy(
            src_ref=picked.at[k], dst_ref=sel.at[at], send_sem=sel_send.at[k],
            recv_sem=sel_recv.at[count - 1 - k], device_id={"blk": region}, device_id_type=MESH,
        )
        copy.start()
        sel_out.append(copy)

    lane64 = iota((AB, LANES), 1)
    row64 = iota((AB, LANES), 0)
    side = (iota((AB, slots * LANES), 1) // AB) % PAIR
    for j in range(groups):
        if j > 0:
            pat_out[groups - 1 - j].wait_recv()
        for t in range(slots):
            start = pats[j, t:t + 1, :] * AB
            hot_rows = jnp.concatenate(
                [
                    (lane64 + (c * LANES) - start == row64).astype(jnp.float32)
                    for c in range(AUXR // LANES)
                ],
                axis=1,
            ).astype(jnp.bfloat16)
            block = jnp.dot(hot_rows, mcol[...], preferred_element_type=jnp.float32)
            for b in range(PAIR):
                at = (t * PAIR + b) * AB
                m2[j, at:at + AB, :] = jnp.where(side == b, block, 0.0).astype(jnp.bfloat16)

    for k in range(count):
        pltpu.make_async_remote_copy(
            src_ref=picked.at[k], dst_ref=sel.at[REACH + NEAR[k]], send_sem=sel_send.at[k],
            recv_sem=sel_recv.at[k], device_id={"blk": near[k]}, device_id_type=MESH,
        ).wait_recv()
    tiles = []
    for t in range(slots):
        source = lax.rem(pat[t, 0, 0] - me + (regions + REACH), regions)
        place = source * (rows // BF) + pat[t, 0, 1]
        evens = jnp.zeros((OSUP, LANES), jnp.float32)
        odds = evens
        for w in range(count + 1):
            for c in range(rows // LANES):
                at = w * (rows // BF) + c * PAIR
                part = sel[w, :, c * LANES:(c + 1) * LANES]
                evens = jnp.where(place == at, part, evens)
                odds = jnp.where(place == at + 1, part, odds)
        tiles.append(evens[:, :BF] + odds[:, BF:])
    mix = []
    for t in range(slots):
        first = jnp.float32(1.0)
        for u in range(t):
            first = jnp.where(aux[u] == aux[t], jnp.float32(0.0), first)
        line = []
        for u in range(slots):
            live = pat[u, 0, 3].astype(jnp.float32)
            line.append(tiles[u] * (jnp.where(aux[u] == aux[t], live, jnp.float32(0.0)) * first))
        mix.append(jnp.concatenate(line, axis=1))
    mix = jnp.concatenate(mix, axis=0).astype(jnp.bfloat16)
    for load in loads[2:]:
        load.wait()
    width = 512
    for n in range(ints.shape[1] // width):
        part = jnp.dot(mix, ints[:, n * width:(n + 1) * width], preferred_element_type=jnp.float32)
        for c in range(width // LANES):
            at = (n * (width // LANES) + c) * OSUP
            for t in range(slots):
                comp[t, at:at + OSUP, :] = part[
                    t * OSUP:(t + 1) * OSUP, c * LANES:(c + 1) * LANES
                ]

    pairs = BF // PAIR
    low = iota((pairs, LANES), 1) < AB
    half_out = []
    for t in range(slots):
        for i in range(HALF):
            at = (t * HALF + i) * BF
            a = comp[t, pl.ds(i, pairs, stride=OSUP), :]
            b = comp[t, pl.ds(i + HALF, pairs, stride=OSUP), :]
            mixed[pl.ds(at, pairs, stride=PAIR), :] = jnp.where(low, a, pltpu.roll(b, AB, 1))
            mixed[pl.ds(at + 1, pairs, stride=PAIR), :] = jnp.where(low, pltpu.roll(a, AB, 1), b)
        span = pl.ds(t * HALF * BF, HALF * BF)
        half[mine, span, :] = mixed[span, :].astype(jnp.bfloat16)
        for j, peer in enumerate(peers):
            copy = pltpu.make_async_remote_copy(
                src_ref=half.at[mine, span], dst_ref=half.at[mine, span],
                send_sem=half_send.at[t, j], recv_sem=half_recv.at[t, groups - 2 - j],
                device_id={"grp": peer}, device_id_type=MESH,
            )
            copy.start()
            half_out.append(copy)

    own = jnp.concatenate(
        [half[mine, pl.ds(t * HALF * BF, HALF * BF), :] for t in range(slots)], axis=1
    )

    def against(j, t, other):
        left = jnp.concatenate(
            [
                kbuf[j, i * BF:(i + 1) * BF, t * LANES:(t + 1) * LANES]
                for i in range(HALF)
            ],
            axis=1,
        )
        right = jnp.concatenate(
            [
                half[other, pl.ds((t * HALF + i) * BF, BF), :]
                for i in range(HALF)
            ],
            axis=1,
        )
        return lax.dot_general(left, right, NT_DIMS, preferred_element_type=jnp.float32)

    for j in range(groups):
        kbuf[j] = lax.dot_general(
            own, m2[j], NT_DIMS, preferred_element_type=jnp.float32
        ).astype(jnp.bfloat16)
    blocks[0] = sum(against(0, t, mine) for t in range(slots))
    for j in range(1, groups):
        other = lax.rem(mine + j, groups)
        total = None
        for t in range(slots):
            span = pl.ds(t * HALF * BF, HALF * BF)
            pltpu.make_async_remote_copy(
                src_ref=half.at[mine, span], dst_ref=half.at[other, span],
                send_sem=half_send.at[t, j - 1], recv_sem=half_recv.at[t, j - 1],
                device_id={"grp": peers[j - 1]}, device_id_type=MESH,
            ).wait_recv()
            term = against(j, t, other)
            total = term if total is None else total + term
        blocks[j] = total
    out_ref[...] = jnp.concatenate(
        [blocks[lax.rem(h - mine + groups, groups)] for h in range(groups)], axis=1
    )
    for copy in sup_out + pat_out + sel_out + half_out:
        copy.wait_send()


def per_device(regions, groups, occupied, integrals, metric_inv, pattern, support):
    rows = occupied.shape[0]
    slots = integrals.shape[2]
    count = len(NEAR)
    tall = slots * OSUP * BF // PAIR
    dma = pltpu.SemaphoreType.DMA
    return pl.pallas_call(
        functools.partial(kernel, regions, groups),
        out_shape=jax.ShapeDtypeStruct((BF, groups * BF), jnp.float32),
        in_specs=[pl.BlockSpec(memory_space=pl.ANY)] * 3
        + [pl.BlockSpec(memory_space=pltpu.SMEM)] * 2,
        out_specs=pl.BlockSpec(memory_space=pltpu.VMEM),
        scratch_shapes=[
            pltpu.VMEM(occupied.shape, jnp.bfloat16),
            pltpu.VMEM((slots * BF, integrals.shape[4]), jnp.bfloat16),
            pltpu.VMEM(metric_inv.shape, jnp.bfloat16),
            pltpu.VMEM((AUXR, slots * LANES), jnp.bfloat16),
            pltpu.VMEM((groups, slots * LANES, slots * LANES), jnp.bfloat16),
            pltpu.VMEM((groups, HALF * BF, slots * LANES), jnp.bfloat16),
            pltpu.VMEM((8, LANES), jnp.int32),
            pltpu.VMEM((8, LANES), jnp.int32),
            pltpu.VMEM((count, 8, LANES), jnp.int32),
            pltpu.VMEM((groups, 8, LANES), jnp.int32),
            pltpu.VMEM((count, OSUP, rows), jnp.float32),
            pltpu.VMEM((count + 1, OSUP, rows), jnp.float32),
            pltpu.VMEM((slots, OSUP * BF // PAIR, LANES), jnp.float32),
            pltpu.VMEM((tall, LANES), jnp.float32),
            pltpu.VMEM((groups, tall, LANES), jnp.bfloat16),
            pltpu.VMEM((groups, BF, BF), jnp.float32),
            dma((2 + slots,)),
            dma((count,)),
            dma((count,)),
            dma((groups - 1,)),
            dma((groups - 1,)),
            dma((count,)),
            dma((count,)),
            dma((slots, groups - 1)),
            dma((slots, groups - 1)),
        ],
        compiler_params=pltpu.CompilerParams(
            collective_id=0, has_side_effects=True, vmem_limit_bytes=62 * 1024 * 1024
        ),
        cost_estimate=pl.CostEstimate(flops=2 * 10**9, bytes_accessed=4 * 10**6, transcendentals=0),
    )(occupied, integrals, metric_inv, pattern.reshape(slots, 1, pattern.shape[3]), support)


def solution(mesh):
    placed = (
        P("blk", None),
        P("blk", "grp", None, None, None),
        P("blk", None),
        P("blk", "grp", None, None),
        P("blk", None),
    )
    return jax.shard_map(
        functools.partial(per_device, mesh.shape["blk"], mesh.shape["grp"]),
        mesh=mesh, in_specs=placed, out_specs=P(("blk", "grp"), None), check_vma=False,
    )
```

```python
import functools

import jax
import jax.numpy as jnp
from jax import lax
from jax.experimental import pallas as pl
from jax.experimental.pallas import tpu as pltpu
from jax.sharding import PartitionSpec as P

BF = 64
AB = 64
AUXR = 1024
OSUP = 8
REACH = 3
LANES = 128
PAIR = LANES // BF
HALF = OSUP // PAIR
NEAR = tuple(d for d in range(-REACH, REACH + 1) if d != 0)
MESH = pl.DeviceIdType.MESH
NT_DIMS = (((1,), (1,)), ((), ()))


def iota(shape, dim):
    return lax.broadcasted_iota(jnp.int32, shape, dim)


def splat_rows(values):
    rows = iota((8, LANES), 0)
    tile = jnp.zeros((8, LANES), jnp.int32)
    for at, value in enumerate(values):
        tile = jnp.where(rows == at, value, tile)
    return tile


def kernel(
    regions, groups, occ_hbm, int_hbm, met_hbm, pat_hbm, sup_hbm, out_ref,
    pat, sup, occ, ints, met, mcol, m2, kbuf, my_sup, my_pat, sups, pats, picked, sel,
    comp, mixed, half, blocks,
    field_sem, load_sem, sup_send, sup_recv, pat_send, pat_recv, sel_send, sel_recv, half_send, half_recv,
):
    slots = int_hbm.shape[2]
    rows = occ.shape[0]
    me = lax.axis_index("blk")
    mine = lax.axis_index("grp")
    near = [lax.rem(me + (d + regions), regions) for d in NEAR]
    peers = [lax.rem(mine + j, groups) for j in range(1, groups)]
    count = len(NEAR)

    loads = [
        pltpu.make_async_copy(occ_hbm, occ, load_sem.at[0]),
        pltpu.make_async_copy(met_hbm, met, load_sem.at[1]),
    ]
    for t in range(slots):
        loads.append(
            pltpu.make_async_copy(int_hbm.at[0, 0, t], ints.at[pl.ds(t * BF, BF)], load_sem.at[2 + t])
        )

    fields = pltpu.make_async_copy(pat_hbm, pat, field_sem.at[0])
    orbitals = pltpu.make_async_copy(sup_hbm, sup, field_sem.at[1])

    barrier = pltpu.get_barrier_semaphore()
    for region in near:
        pl.semaphore_signal(barrier, inc=1, device_id={"blk": region}, device_id_type=MESH)
    for peer in peers:
        pl.semaphore_signal(barrier, inc=1, device_id={"grp": peer}, device_id_type=MESH)
    orbitals.start()
    fields.start()
    for load in loads:
        load.start()
    orbitals.wait()
    fields.wait()

    aux = [pat[t, 0, 2] for t in range(slots)]
    my_sup[...] = splat_rows([sup[0, i] for i in range(OSUP)])
    my_pat[...] = splat_rows(aux)
    pats[0] = my_pat[...]
    pl.semaphore_wait(barrier, count + groups - 1)

    sup_out, pat_out = [], []
    for k, region in enumerate(near):
        copy = pltpu.make_async_remote_copy(
            src_ref=my_sup, dst_ref=sups.at[count - 1 - k], send_sem=sup_send.at[k],
            recv_sem=sup_recv.at[count - 1 - k], device_id={"blk": region}, device_id_type=MESH,
        )
        copy.start()
        sup_out.append(copy)
    for j, peer in enumerate(peers):
        copy = pltpu.make_async_remote_copy(
            src_ref=my_pat, dst_ref=pats.at[groups - 1 - j], send_sem=pat_send.at[j],
            recv_sem=pat_recv.at[groups - 2 - j], device_id={"grp": peer}, device_id_type=MESH,
        )
        copy.start()
        pat_out.append(copy)

    loads[1].wait()
    tall = iota((AUXR, LANES), 0)
    wide = iota((1, LANES), 1) % AB
    pick = jnp.concatenate(
        [(tall == aux[t] * AB + wide).astype(jnp.float32) for t in range(slots)], axis=1
    ).astype(jnp.bfloat16)
    mcol[...] = jnp.dot(met[...], pick, preferred_element_type=jnp.float32).astype(jnp.bfloat16)

    def one_hot(tile):
        lane = iota((8, LANES), 1)
        parts = [(lane + c * LANES == tile).astype(jnp.float32) for c in range(occ.shape[1] // LANES)]
        return jnp.concatenate(parts, axis=1)

    loads[0].wait()
    for k in range(count):
        sup_out[k].wait_recv()
    hot = jnp.concatenate([one_hot(sups[k]) for k in range(count)] + [one_hot(my_sup[...])], axis=0)
    chosen = lax.dot_general(
        hot.astype(jnp.bfloat16), occ[...], NT_DIMS, preferred_element_type=jnp.float32
    )
    for k in range(count):
        picked[k] = chosen[k * OSUP:(k + 1) * OSUP]
    sel[REACH] = chosen[count * OSUP:(count + 1) * OSUP]
    sel_out = []
    for k, region in enumerate(near):
        at = REACH - NEAR[k]
        copy = pltpu.make_async_remote_copy(
            src_ref=picked.at[k], dst_ref=sel.at[at], send_sem=sel_send.at[k],
            recv_sem=sel_recv.at[count - 1 - k], device_id={"blk": region}, device_id_type=MESH,
        )
        copy.start()
        sel_out.append(copy)

    lane64 = iota((AB, LANES), 1)
    row64 = iota((AB, LANES), 0)
    side = (iota((AB, slots * LANES), 1) // AB) % PAIR
    for j in range(groups):
        if j > 0:
            pat_out[groups - 1 - j].wait_recv()
        for t in range(slots):
            start = pats[j, t:t + 1, :] * AB
            hot_rows = jnp.concatenate(
                [
                    (lane64 + (c * LANES) - start == row64).astype(jnp.float32)
                    for c in range(AUXR // LANES)
                ],
                axis=1,
            ).astype(jnp.bfloat16)
            block = jnp.dot(hot_rows, mcol[...], preferred_element_type=jnp.float32)
            for b in range(PAIR):
                at = (t * PAIR + b) * AB
                m2[j, at:at + AB, :] = jnp.where(side == b, block, 0.0).astype(jnp.bfloat16)

    for k in range(count):
        pltpu.make_async_remote_copy(
            src_ref=picked.at[k], dst_ref=sel.at[REACH + NEAR[k]], send_sem=sel_send.at[k],
            recv_sem=sel_recv.at[k], device_id={"blk": near[k]}, device_id_type=MESH,
        ).wait_recv()
    tiles = []
    for t in range(slots):
        source = lax.rem(pat[t, 0, 0] - me + (regions + REACH), regions)
        place = source * (rows // BF) + pat[t, 0, 1]
        evens = jnp.zeros((OSUP, LANES), jnp.float32)
        odds = evens
        for w in range(count + 1):
            for c in range(rows // LANES):
                at = w * (rows // BF) + c * PAIR
                part = sel[w, :, c * LANES:(c + 1) * LANES]
                evens = jnp.where(place == at, part, evens)
                odds = jnp.where(place == at + 1, part, odds)
        tiles.append(evens[:, :BF] + odds[:, BF:])
    mix = []
    for t in range(slots):
        first = jnp.float32(1.0)
        for u in range(t):
            first = jnp.where(aux[u] == aux[t], jnp.float32(0.0), first)
        line = []
        for u in range(slots):
            live = pat[u, 0, 3].astype(jnp.float32)
            line.append(tiles[u] * (jnp.where(aux[u] == aux[t], live, jnp.float32(0.0)) * first))
        mix.append(jnp.concatenate(line, axis=1))
    mix = jnp.concatenate(mix, axis=0).astype(jnp.bfloat16)
    for load in loads[2:]:
        load.wait()
    width = 512
    for n in range(ints.shape[1] // width):
        part = jnp.dot(mix, ints[:, n * width:(n + 1) * width], preferred_element_type=jnp.float32)
        for c in range(width // LANES):
            at = (n * (width // LANES) + c) * OSUP
            for t in range(slots):
                comp[t, at:at + OSUP, :] = part[
                    t * OSUP:(t + 1) * OSUP, c * LANES:(c + 1) * LANES
                ]

    pairs = BF // PAIR
    low = iota((pairs, LANES), 1) < AB
    half_out = []
    for t in range(slots):
        for i in range(HALF):
            at = (t * HALF + i) * BF
            a = comp[t, pl.ds(i, pairs, stride=OSUP), :]
            b = comp[t, pl.ds(i + HALF, pairs, stride=OSUP), :]
            mixed[pl.ds(at, pairs, stride=PAIR), :] = jnp.where(low, a, pltpu.roll(b, AB, 1))
            mixed[pl.ds(at + 1, pairs, stride=PAIR), :] = jnp.where(low, pltpu.roll(a, AB, 1), b)
        span = pl.ds(t * HALF * BF, HALF * BF)
        half[mine, span, :] = mixed[span, :].astype(jnp.bfloat16)
        for j, peer in enumerate(peers):
            copy = pltpu.make_async_remote_copy(
                src_ref=half.at[mine, span], dst_ref=half.at[mine, span],
                send_sem=half_send.at[t, j], recv_sem=half_recv.at[t, groups - 2 - j],
                device_id={"grp": peer}, device_id_type=MESH,
            )
            copy.start()
            half_out.append(copy)

    own = jnp.concatenate(
        [half[mine, pl.ds(t * HALF * BF, HALF * BF), :] for t in range(slots)], axis=1
    )

    def against(j, t, other):
        left = jnp.concatenate(
            [
                kbuf[j, i * BF:(i + 1) * BF, t * LANES:(t + 1) * LANES]
                for i in range(HALF)
            ],
            axis=1,
        )
        right = jnp.concatenate(
            [
                half[other, pl.ds((t * HALF + i) * BF, BF), :]
                for i in range(HALF)
            ],
            axis=1,
        )
        return lax.dot_general(left, right, NT_DIMS, preferred_element_type=jnp.float32)

    for j in range(groups):
        kbuf[j] = lax.dot_general(
            own, m2[j], NT_DIMS, preferred_element_type=jnp.float32
        ).astype(jnp.bfloat16)
    blocks[0] = sum(against(0, t, mine) for t in range(slots))
    for j in range(1, groups):
        other = lax.rem(mine + j, groups)
        total = None
        for t in range(slots):
            span = pl.ds(t * HALF * BF, HALF * BF)
            pltpu.make_async_remote_copy(
                src_ref=half.at[mine, span], dst_ref=half.at[other, span],
                send_sem=half_send.at[t, j - 1], recv_sem=half_recv.at[t, j - 1],
                device_id={"grp": peers[j - 1]}, device_id_type=MESH,
            ).wait_recv()
            term = against(j, t, other)
            total = term if total is None else total + term
        blocks[j] = total
    out_ref[...] = jnp.concatenate(
        [blocks[lax.rem(h - mine + groups, groups)] for h in range(groups)], axis=1
    )
    for copy in sup_out + pat_out + sel_out + half_out:
        copy.wait_send()


def per_device(regions, groups, occupied, integrals, metric_inv, pattern, support):
    rows = occupied.shape[0]
    slots = integrals.shape[2]
    count = len(NEAR)
    tall = slots * OSUP * BF // PAIR
    dma = pltpu.SemaphoreType.DMA
    return pl.pallas_call(
        functools.partial(kernel, regions, groups),
        out_shape=jax.ShapeDtypeStruct((BF, groups * BF), jnp.float32),
        in_specs=[pl.BlockSpec(memory_space=pl.ANY)] * 5,
        out_specs=pl.BlockSpec(memory_space=pltpu.VMEM),
        scratch_shapes=[
            pltpu.SMEM((slots, 1, pattern.shape[3]), jnp.int32),
            pltpu.SMEM(support.shape, jnp.int32),
            pltpu.VMEM(occupied.shape, jnp.bfloat16),
            pltpu.VMEM((slots * BF, integrals.shape[4]), jnp.bfloat16),
            pltpu.VMEM(metric_inv.shape, jnp.bfloat16),
            pltpu.VMEM((AUXR, slots * LANES), jnp.bfloat16),
            pltpu.VMEM((groups, slots * LANES, slots * LANES), jnp.bfloat16),
            pltpu.VMEM((groups, HALF * BF, slots * LANES), jnp.bfloat16),
            pltpu.VMEM((8, LANES), jnp.int32),
            pltpu.VMEM((8, LANES), jnp.int32),
            pltpu.VMEM((count, 8, LANES), jnp.int32),
            pltpu.VMEM((groups, 8, LANES), jnp.int32),
            pltpu.VMEM((count, OSUP, rows), jnp.float32),
            pltpu.VMEM((count + 1, OSUP, rows), jnp.float32),
            pltpu.VMEM((slots, OSUP * BF // PAIR, LANES), jnp.float32),
            pltpu.VMEM((tall, LANES), jnp.float32),
            pltpu.VMEM((groups, tall, LANES), jnp.bfloat16),
            pltpu.VMEM((groups, BF, BF), jnp.float32),
            dma((2,)),
            dma((2 + slots,)),
            dma((count,)),
            dma((count,)),
            dma((groups - 1,)),
            dma((groups - 1,)),
            dma((count,)),
            dma((count,)),
            dma((slots, groups - 1)),
            dma((slots, groups - 1)),
        ],
        compiler_params=pltpu.CompilerParams(
            collective_id=0, has_side_effects=True, vmem_limit_bytes=62 * 1024 * 1024
        ),
        cost_estimate=pl.CostEstimate(flops=2 * 10**9, bytes_accessed=4 * 10**6, transcendentals=0),
    )(occupied, integrals, metric_inv, pattern.reshape(slots, 1, pattern.shape[3]), support)


def solution(mesh):
    placed = (
        P("blk", None),
        P("blk", "grp", None, None, None),
        P("blk", None),
        P("blk", "grp", None, None),
        P("blk", None),
    )
    return jax.shard_map(
        functools.partial(per_device, mesh.shape["blk"], mesh.shape["grp"]),
        mesh=mesh, in_specs=placed, out_specs=P(("blk", "grp"), None), check_vma=False,
    )
```

```python
import functools

import jax
import jax.numpy as jnp
from jax import lax
from jax.experimental import pallas as pl
from jax.experimental.pallas import tpu as pltpu
from jax.sharding import PartitionSpec as P

BF = 64
AB = 64
AUXR = 1024
OSUP = 8
REACH = 3
LANES = 128
PAIR = LANES // BF
HALF = OSUP // PAIR
NEAR = tuple(d for d in range(-REACH, REACH + 1) if d != 0)
MESH = pl.DeviceIdType.MESH
NT_DIMS = (((1,), (1,)), ((), ()))


def iota(shape, dim):
    return lax.broadcasted_iota(jnp.int32, shape, dim)


def splat_rows(values):
    rows = iota((8, LANES), 0)
    tile = jnp.zeros((8, LANES), jnp.int32)
    for at, value in enumerate(values):
        tile = jnp.where(rows == at, value, tile)
    return tile


def kernel(
    regions, groups, occ_hbm, int_hbm, met_hbm, pat_hbm, sup_hbm, out_ref,
    pat, sup, occ, ints, met, mcol, m2, kbuf, my_sup, my_pat, sups, pats, picked, sel,
    comp, mixed, half, blocks,
    field_sem, load_sem, sup_send, sup_recv, pat_send, pat_recv, sel_send, sel_recv, half_send, half_recv,
):
    slots = int_hbm.shape[2]
    rows = occ.shape[0]
    me = lax.axis_index("blk")
    mine = lax.axis_index("grp")
    near = [lax.rem(me + (d + regions), regions) for d in NEAR]
    peers = [lax.rem(mine + j, groups) for j in range(1, groups)]
    count = len(NEAR)

    loads = [
        pltpu.make_async_copy(occ_hbm, occ, load_sem.at[0]),
        pltpu.make_async_copy(met_hbm, met, load_sem.at[1]),
    ]
    for t in range(slots):
        loads.append(
            pltpu.make_async_copy(int_hbm.at[0, 0, t], ints.at[pl.ds(t * BF, BF)], load_sem.at[2 + t])
        )

    fields = pltpu.make_async_copy(pat_hbm, pat, field_sem.at[0])
    orbitals = pltpu.make_async_copy(sup_hbm, sup, field_sem.at[1])

    barrier = pltpu.get_barrier_semaphore()
    for region in near[::-1]:
        pl.semaphore_signal(barrier, inc=1, device_id={"blk": region}, device_id_type=MESH)
    for peer in peers:
        pl.semaphore_signal(barrier, inc=1, device_id={"grp": peer}, device_id_type=MESH)
    orbitals.start()
    fields.start()
    for load in loads:
        load.start()
    orbitals.wait()
    fields.wait()

    aux = [pat[t, 0, 2] for t in range(slots)]
    my_sup[...] = splat_rows([sup[0, i] for i in range(OSUP)])
    my_pat[...] = splat_rows(aux)
    pats[0] = my_pat[...]
    pl.semaphore_wait(barrier, count + groups - 1)

    sup_out, pat_out = [], []
    for k, region in enumerate(near):
        copy = pltpu.make_async_remote_copy(
            src_ref=my_sup, dst_ref=sups.at[count - 1 - k], send_sem=sup_send.at[k],
            recv_sem=sup_recv.at[count - 1 - k], device_id={"blk": region}, device_id_type=MESH,
        )
        copy.start()
        sup_out.append(copy)
    for j, peer in enumerate(peers):
        copy = pltpu.make_async_remote_copy(
            src_ref=my_pat, dst_ref=pats.at[groups - 1 - j], send_sem=pat_send.at[j],
            recv_sem=pat_recv.at[groups - 2 - j], device_id={"grp": peer}, device_id_type=MESH,
        )
        copy.start()
        pat_out.append(copy)

    loads[1].wait()
    tall = iota((AUXR, LANES), 0)
    wide = iota((1, LANES), 1) % AB
    pick = jnp.concatenate(
        [(tall == aux[t] * AB + wide).astype(jnp.float32) for t in range(slots)], axis=1
    ).astype(jnp.bfloat16)
    mcol[...] = jnp.dot(met[...], pick, preferred_element_type=jnp.float32).astype(jnp.bfloat16)

    def one_hot(tile):
        lane = iota((8, LANES), 1)
        parts = [(lane + c * LANES == tile).astype(jnp.float32) for c in range(occ.shape[1] // LANES)]
        return jnp.concatenate(parts, axis=1)

    loads[0].wait()
    for k in range(count):
        sup_out[k].wait_recv()
    hot = jnp.concatenate([one_hot(sups[k]) for k in range(count)] + [one_hot(my_sup[...])], axis=0)
    chosen = lax.dot_general(
        hot.astype(jnp.bfloat16), occ[...], NT_DIMS, preferred_element_type=jnp.float32
    )
    for k in range(count):
        picked[k] = chosen[k * OSUP:(k + 1) * OSUP]
    sel[REACH] = chosen[count * OSUP:(count + 1) * OSUP]
    sel_out = []
    for k, region in reversed(list(enumerate(near))):
        at = REACH - NEAR[k]
        copy = pltpu.make_async_remote_copy(
            src_ref=picked.at[k], dst_ref=sel.at[at], send_sem=sel_send.at[k],
            recv_sem=sel_recv.at[count - 1 - k], device_id={"blk": region}, device_id_type=MESH,
        )
        copy.start()
        sel_out.append(copy)

    lane64 = iota((AB, LANES), 1)
    row64 = iota((AB, LANES), 0)
    side = (iota((AB, slots * LANES), 1) // AB) % PAIR
    for j in range(groups):
        if j > 0:
            pat_out[groups - 1 - j].wait_recv()
        for t in range(slots):
            start = pats[j, t:t + 1, :] * AB
            hot_rows = jnp.concatenate(
                [
                    (lane64 + (c * LANES) - start == row64).astype(jnp.float32)
                    for c in range(AUXR // LANES)
                ],
                axis=1,
            ).astype(jnp.bfloat16)
            block = jnp.dot(hot_rows, mcol[...], preferred_element_type=jnp.float32)
            for b in range(PAIR):
                at = (t * PAIR + b) * AB
                m2[j, at:at + AB, :] = jnp.where(side == b, block, 0.0).astype(jnp.bfloat16)

    for k in range(count):
        pltpu.make_async_remote_copy(
            src_ref=picked.at[k], dst_ref=sel.at[REACH + NEAR[k]], send_sem=sel_send.at[k],
            recv_sem=sel_recv.at[k], device_id={"blk": near[k]}, device_id_type=MESH,
        ).wait_recv()
    tiles = []
    for t in range(slots):
        source = lax.rem(pat[t, 0, 0] - me + (regions + REACH), regions)
        place = source * (rows // BF) + pat[t, 0, 1]
        evens = jnp.zeros((OSUP, LANES), jnp.float32)
        odds = evens
        for w in range(count + 1):
            for c in range(rows // LANES):
                at = w * (rows // BF) + c * PAIR
                part = sel[w, :, c * LANES:(c + 1) * LANES]
                evens = jnp.where(place == at, part, evens)
                odds = jnp.where(place == at + 1, part, odds)
        tiles.append(evens[:, :BF] + odds[:, BF:])
    mix = []
    for t in range(slots):
        first = jnp.float32(1.0)
        for u in range(t):
            first = jnp.where(aux[u] == aux[t], jnp.float32(0.0), first)
        line = []
        for u in range(slots):
            live = pat[u, 0, 3].astype(jnp.float32)
            line.append(tiles[u] * (jnp.where(aux[u] == aux[t], live, jnp.float32(0.0)) * first))
        mix.append(jnp.concatenate(line, axis=1))
    mix = jnp.concatenate(mix, axis=0).astype(jnp.bfloat16)
    for load in loads[2:]:
        load.wait()
    width = 512
    for n in range(ints.shape[1] // width):
        part = jnp.dot(mix, ints[:, n * width:(n + 1) * width], preferred_element_type=jnp.float32)
        for c in range(width // LANES):
            at = (n * (width // LANES) + c) * OSUP
            for t in range(slots):
                comp[t, at:at + OSUP, :] = part[
                    t * OSUP:(t + 1) * OSUP, c * LANES:(c + 1) * LANES
                ]

    pairs = BF // PAIR
    low = iota((pairs, LANES), 1) < AB
    half_out = []
    for t in range(slots):
        for i in range(HALF):
            at = (t * HALF + i) * BF
            a = comp[t, pl.ds(i, pairs, stride=OSUP), :]
            b = comp[t, pl.ds(i + HALF, pairs, stride=OSUP), :]
            mixed[pl.ds(at, pairs, stride=PAIR), :] = jnp.where(low, a, pltpu.roll(b, AB, 1))
            mixed[pl.ds(at + 1, pairs, stride=PAIR), :] = jnp.where(low, pltpu.roll(a, AB, 1), b)
        span = pl.ds(t * HALF * BF, HALF * BF)
        half[mine, span, :] = mixed[span, :].astype(jnp.bfloat16)
        for j, peer in enumerate(peers):
            copy = pltpu.make_async_remote_copy(
                src_ref=half.at[mine, span], dst_ref=half.at[mine, span],
                send_sem=half_send.at[t, j], recv_sem=half_recv.at[t, groups - 2 - j],
                device_id={"grp": peer}, device_id_type=MESH,
            )
            copy.start()
            half_out.append(copy)

    own = jnp.concatenate(
        [half[mine, pl.ds(t * HALF * BF, HALF * BF), :] for t in range(slots)], axis=1
    )

    def against(j, t, other):
        left = jnp.concatenate(
            [
                kbuf[j, i * BF:(i + 1) * BF, t * LANES:(t + 1) * LANES]
                for i in range(HALF)
            ],
            axis=1,
        )
        right = jnp.concatenate(
            [
                half[other, pl.ds((t * HALF + i) * BF, BF), :]
                for i in range(HALF)
            ],
            axis=1,
        )
        return lax.dot_general(left, right, NT_DIMS, preferred_element_type=jnp.float32)

    for j in range(groups):
        kbuf[j] = lax.dot_general(
            own, m2[j], NT_DIMS, preferred_element_type=jnp.float32
        ).astype(jnp.bfloat16)
    blocks[0] = sum(against(0, t, mine) for t in range(slots))
    for j in range(1, groups):
        other = lax.rem(mine + j, groups)
        total = None
        for t in range(slots):
            span = pl.ds(t * HALF * BF, HALF * BF)
            pltpu.make_async_remote_copy(
                src_ref=half.at[mine, span], dst_ref=half.at[other, span],
                send_sem=half_send.at[t, j - 1], recv_sem=half_recv.at[t, j - 1],
                device_id={"grp": peers[j - 1]}, device_id_type=MESH,
            ).wait_recv()
            term = against(j, t, other)
            total = term if total is None else total + term
        blocks[j] = total
    out_ref[...] = jnp.concatenate(
        [blocks[lax.rem(h - mine + groups, groups)] for h in range(groups)], axis=1
    )
    for copy in sup_out + pat_out + sel_out + half_out:
        copy.wait_send()


def per_device(regions, groups, occupied, integrals, metric_inv, pattern, support):
    rows = occupied.shape[0]
    slots = integrals.shape[2]
    count = len(NEAR)
    tall = slots * OSUP * BF // PAIR
    dma = pltpu.SemaphoreType.DMA
    return pl.pallas_call(
        functools.partial(kernel, regions, groups),
        out_shape=jax.ShapeDtypeStruct((BF, groups * BF), jnp.float32),
        in_specs=[pl.BlockSpec(memory_space=pl.ANY)] * 5,
        out_specs=pl.BlockSpec(memory_space=pltpu.VMEM),
        scratch_shapes=[
            pltpu.SMEM((slots, 1, pattern.shape[3]), jnp.int32),
            pltpu.SMEM(support.shape, jnp.int32),
            pltpu.VMEM(occupied.shape, jnp.bfloat16),
            pltpu.VMEM((slots * BF, integrals.shape[4]), jnp.bfloat16),
            pltpu.VMEM(metric_inv.shape, jnp.bfloat16),
            pltpu.VMEM((AUXR, slots * LANES), jnp.bfloat16),
            pltpu.VMEM((groups, slots * LANES, slots * LANES), jnp.bfloat16),
            pltpu.VMEM((groups, HALF * BF, slots * LANES), jnp.bfloat16),
            pltpu.VMEM((8, LANES), jnp.int32),
            pltpu.VMEM((8, LANES), jnp.int32),
            pltpu.VMEM((count, 8, LANES), jnp.int32),
            pltpu.VMEM((groups, 8, LANES), jnp.int32),
            pltpu.VMEM((count, OSUP, rows), jnp.float32),
            pltpu.VMEM((count + 1, OSUP, rows), jnp.float32),
            pltpu.VMEM((slots, OSUP * BF // PAIR, LANES), jnp.float32),
            pltpu.VMEM((tall, LANES), jnp.float32),
            pltpu.VMEM((groups, tall, LANES), jnp.bfloat16),
            pltpu.VMEM((groups, BF, BF), jnp.float32),
            dma((2,)),
            dma((2 + slots,)),
            dma((count,)),
            dma((count,)),
            dma((groups - 1,)),
            dma((groups - 1,)),
            dma((count,)),
            dma((count,)),
            dma((slots, groups - 1)),
            dma((slots, groups - 1)),
        ],
        compiler_params=pltpu.CompilerParams(
            collective_id=0, has_side_effects=True, vmem_limit_bytes=62 * 1024 * 1024
        ),
        cost_estimate=pl.CostEstimate(flops=2 * 10**9, bytes_accessed=4 * 10**6, transcendentals=0),
    )(occupied, integrals, metric_inv, pattern.reshape(slots, 1, pattern.shape[3]), support)


def solution(mesh):
    placed = (
        P("blk", None),
        P("blk", "grp", None, None, None),
        P("blk", None),
        P("blk", "grp", None, None),
        P("blk", None),
    )
    return jax.shard_map(
        functools.partial(per_device, mesh.shape["blk"], mesh.shape["grp"]),
        mesh=mesh, in_specs=placed, out_specs=P(("blk", "grp"), None), check_vma=False,
    )
```
